256 devices in a mesh: occ: 64 (over z, y, core), vir: 4 (over x).
Axes of the slice: x: 4, y: 4, z: 8, core: 2. Of those that a mesh axis runs over, the one named last changes fastest.
Arguments:
- chol: bfloat16 [2560, 128, 1408], P('occ', None, 'vir'), may hold values from -0.125 to 0.125
- dressed: bfloat16 [2560, 128, 1408], P('occ', None, 'vir'), may hold values from -6 to 6
- pair_mask: int32 [128, 128], replicated, may hold values 0 or 1
- sym_mask: int32 [88, 88], replicated, may hold values 0 or 1
Outputs:
- residual: bfloat16 [128, 2, 1408, 1408], P('occ', None, 'vir')
The draws below stay inside these ranges and needn't reach their ends.
All inputs are finite; a program needn't handle non-finite values.
Results may differ from the reference program's by a relative error of at most 0.0051.
Values may be sent and summed in bfloat16 or wider, within the bound.
No kernel may reach another device: no remote copies, remote signals or barrier semaphores. Data moves between devices by JAX's collectives and lax.ppermute only.
A program may use at most 128 MiB of HBM per device.

```python
import jax
import jax.numpy as jnp
from jax import lax

NAUX = 2560
V = 1408
SLAB = 16
O = 128
NB = 88
N_OCC = 64


def plant(values, stream_key, least, high):
    extent = values.shape
    place = [jax.random.randint(jax.random.fold_in(stream_key, axis), (), 0, extent[axis]) for axis in range(len(extent))]
    values = values.at[tuple(place)].set(least)
    longest = extent.index(max(extent))
    place[longest] = (place[longest] + 1) % extent[longest]
    return values.at[tuple(place)].set(high)


def shard_levels(key, dims, split, low, largest):
    factor_of, own = 1.0, jax.random.fold_in(key, 6)
    for axis_at, parts in split:
        draws = jnp.exp(jax.random.uniform(jax.random.fold_in(own, axis_at), (parts,), jnp.float32, low / len(split), largest / len(split)))
        factor_of = factor_of * jnp.repeat(draws, dims[axis_at] // parts).reshape([-1 if axis == axis_at else 1 for axis in range(len(dims))])
    return factor_of


def centred(stream_key, extent, scale, most, pieces=(), kind=jnp.bfloat16):
    values = jax.random.normal(stream_key, extent, jnp.float32) * scale
    if len(pieces) > 0:
        values = shard_levels(stream_key, extent, pieces, -0.22, 0.18) * values
    return jnp.clip(values, min=-most, max=most).astype(kind)


def setup_inputs(seed: int = 0) -> dict:
    arg_keys = jax.random.split(jax.random.key(seed), 5)
    return {
        "chol": centred(arg_keys[0], (NAUX, O, V), NAUX ** -0.5, 0.125, ((0, 64), (2, 4))),
        "dressed": centred(arg_keys[1], (NAUX, O, V), 1.0, 6.0, ((0, 64), (2, 4))),
        "pair_mask": plant((jax.random.randint(arg_keys[2], (O, O), 0, 4) < 3).astype(jnp.int32), jax.random.fold_in(arg_keys[2], 1), 0, 1),
        "sym_mask": plant((jax.random.randint(arg_keys[3], (NB, NB), 0, 2) < 1).astype(jnp.int32), jax.random.fold_in(arg_keys[3], 1), 0, 1),
    }


def reference(chol, dressed, pair_mask, sym_mask):
    width = O // N_OCC
    half = N_OCC // 2
    expand = jnp.repeat(jnp.repeat(sym_mask.astype(jnp.float32), SLAB, 0), SLAB, 1)

    def tile(block):
        mirror = (block + half) % N_OCC
        start = (block * width).astype(jnp.int32)
        far = (mirror * width).astype(jnp.int32)
        own_l = lax.dynamic_slice_in_dim(chol, start, width, 1).astype(jnp.float32)
        own_x = lax.dynamic_slice_in_dim(dressed, start, width, 1).astype(jnp.float32)
        far_l = lax.dynamic_slice_in_dim(chol, far, width, 1).astype(jnp.float32)
        far_x = lax.dynamic_slice_in_dim(dressed, far, width, 1).astype(jnp.float32)
        direct = jnp.einsum("pia,pjb->ijab", own_l, far_x, precision=lax.Precision.HIGHEST).astype(jnp.bfloat16)
        mirrored = jnp.einsum("pjb,pia->ijab", far_l, own_x, precision=lax.Precision.HIGHEST).astype(jnp.bfloat16)
        direct, mirrored = lax.optimization_barrier((direct, mirrored))
        pairs = lax.dynamic_slice(pair_mask, (start, far), (width, width)).astype(jnp.float32)
        total = direct.astype(jnp.float32) + mirrored.astype(jnp.float32)
        return (pairs[:, :, None, None] * expand[None, None] * total).astype(jnp.bfloat16)

    blocks = lax.map(tile, jnp.arange(N_OCC, dtype=jnp.int32))
    return blocks.reshape(O, width, V, V)
```

```python
import functools

import jax
import jax.numpy as jnp
from jax import lax
from jax.experimental import pallas as pl
from jax.experimental.pallas import tpu as pltpu
from jax.sharding import PartitionSpec as P

SLAB = 16
NZ, NY, NC = 8, 4, 2
PLACES = NZ * NY * NC
STEPS = 8
FIRST = 32
ROWS, GROUPS = 16, 4
PARAMS = pltpu.CompilerParams(vmem_limit_bytes=48 * 1024 * 1024)


def place(z, y, c):
    return ((z % NZ) * NY + y) * NC + c


def centres():
    return [place(low + 2 + 4 * c, y, r) for low in range(4) for y in range(NY) for c in range(NC) for r in range(2)]


def core_route():
    return [(place(z, y, c), place(z, y, 1 - c)) for z in range(NZ) for y in range(NY) for c in range(NC)]


def x_route(bits):
    return [(g, g ^ bits) for g in range(4)]


def home_route(first, k_bits, m_bits):
    route = []
    for low in range(4):
        for c in range(NC):
            for y in range(NY):
                for r in range(NC):
                    to_k = (r == 0) == first
                    here, there = place(low + 2 + 4 * c, y, r), place(low if to_k else low + 4, y, c)
                    bits = k_bits if to_k else m_bits
                    route += [(here * 4 + g, there * 4 + (g ^ bits)) for g in range(4)]
    return route


def pack_body(l_ref, x_ref, one_ref, two_ref):
    quarter = l_ref.shape[-1]
    for side in range(2):
        pair = (l_ref, x_ref) if side == 0 else (x_ref, l_ref)
        rows = [ref[side] for ref in pair]
        for at in range(GROUPS):
            from_row = at % 2 * ROWS
            one_ref[:, side, :, at * quarter : (at + 1) * quarter] = rows[at // 2][:, from_row : from_row + ROWS]
        two_ref[:, side] = jnp.concatenate([row[:, FIRST:] for row in rows], axis=1)


def pack(chol, dressed):
    _, width, rows, quarter = chol.shape
    share = width // STEPS
    sizes = [(ROWS, GROUPS * quarter), (2 * (rows - FIRST), quarter)]
    return pl.pallas_call(
        pack_body,
        grid=(STEPS,),
        in_specs=[pl.BlockSpec((2, share, rows, quarter), lambda n: (0, n, 0, 0))] * 2,
        out_specs=[pl.BlockSpec((share, 2, *size), lambda n: (n, 0, 0, 0)) for size in sizes],
        out_shape=[jax.ShapeDtypeStruct((width, 2, *size), jnp.bfloat16) for size in sizes],
        compiler_params=PARAMS,
        name="pack",
    )(chol, dressed)


def split_body(part_ref, after_ref, k_ref, m_ref):
    k_ref[...], m_ref[...] = part_ref[:, 0], part_ref[:, 1]


def split(part, after):
    width, _, rows, lanes = part.shape
    share = width // 4
    half = pl.BlockSpec((share, rows, lanes), lambda n: (n, 0, 0))
    return pl.pallas_call(
        split_body,
        grid=(4,),
        in_specs=[pl.BlockSpec((share, 2, rows, lanes), lambda n: (n, 0, 0, 0)), pl.BlockSpec(memory_space=pl.ANY)],
        out_specs=[half] * 2,
        out_shape=[jax.ShapeDtypeStruct((width, rows, lanes), jnp.bfloat16)] * 2,
        compiler_params=PARAMS,
        name="split",
    )(part, after)


def in_lanes(ref, tiles):
    quarter = tiles[0].shape[1]
    at = 0
    for tile in tiles:
        for half in range(2):
            ref[:, at : at + quarter] = tile[half * quarter // 2 : (half + 1) * quarter // 2]
            at += quarter


def finish_near(core, total, first_ref, second_ref):
    straight = [total[e].astype(jnp.bfloat16) for e in range(2)]
    turned = [total[e].T.astype(jnp.bfloat16) for e in range(2)]

    @pl.when(core == 0)
    def _():
        in_lanes(first_ref, straight)
        in_lanes(second_ref, turned)

    @pl.when(core == 1)
    def _():
        in_lanes(first_ref, turned[::-1])
        in_lanes(second_ref, straight[::-1])


def finish_far(core, total, first_ref, second_ref, first_far, second_far):
    tiles = [[total[3 * e + at].astype(jnp.bfloat16) for e in range(2)] for at in range(3)]
    turned = [[total[3 * e + at].T.astype(jnp.bfloat16) for e in range(2)] for at in range(3)]
    (op, po, pp), (op_t, po_t, pp_t) = tiles, turned

    @pl.when(core == 0)
    def _():
        in_lanes(first_ref, op)
        in_lanes(second_ref, po_t)
        for e in range(2):
            in_lanes(first_far.at[e], (po[e], pp[e]))
            in_lanes(second_far.at[e], (op_t[e], pp_t[e]))

    @pl.when(core == 1)
    def _():
        in_lanes(second_ref, op[::-1])
        in_lanes(first_ref, po_t[::-1])
        for e in range(2):
            in_lanes(second_far.at[1 - e], (po[e], pp[e]))
            in_lanes(first_far.at[1 - e], (op_t[e], pp_t[e]))


def tiles_body(n_ops, combos, carried, finish, core_ref, *refs):
    ops, refs = refs[:n_ops], refs[n_ops:]
    if carried:
        before, refs = refs[0], refs[1:]
    total = refs[-1] if finish else refs[0]
    step = pl.program_id(0)

    @pl.when(step == 0)
    def _():
        total[...] = before[...] if carried else jnp.zeros_like(total)

    quarter = total.shape[-1]
    blocks = []
    for op in ops:
        lanes = [op[:, :, at : at + quarter].reshape(-1, quarter) for at in range(0, op.shape[-1], quarter)]
        blocks.append(lanes[0] if len(lanes) == 1 else jnp.concatenate(lanes, axis=0))
    for at, (left, right) in enumerate(combos):
        total[at] += lax.dot_general(
            blocks[left], blocks[right], (((0,), (0,)), ((), ())), preferred_element_type=jnp.float32
        )
    if finish:

        @pl.when(step == pl.num_programs(0) - 1)
        def _():
            finish(core_ref[0], total, *refs[:-1])


def tiles(name, quarter, core, ops, combos, before=None, finish=None):
    specs, arrays = [], []
    for op in ops:
        array, side = op if isinstance(op, tuple) else (op, None)
        width, rows, lanes = array.shape[0], array.shape[-2], array.shape[-1]
        share = 512 * quarter // (rows * lanes)
        if side is None:
            specs.append(pl.BlockSpec((share, rows, lanes), lambda n: (n, 0, 0)))
        else:
            specs.append(pl.BlockSpec((share, None, rows, lanes), lambda n, s=side: (n, s, 0, 0)))
        arrays.append(array)
    sums = (len(combos), quarter, quarter)
    if before is not None:
        specs.append(pl.BlockSpec(sums, lambda n: (0, 0, 0)))
        arrays.append(before)
    if finish is None:
        shapes, scratch = [sums], []
        kind = jnp.float32
    else:
        near = (quarter // 2, 4 * quarter)
        shapes = [near] * 2 if finish is finish_near else [near] * 2 + [(2,) + near] * 2
        scratch = [pltpu.VMEM(sums, jnp.float32)]
        kind = jnp.bfloat16
    return pl.pallas_call(
        functools.partial(tiles_body, len(ops), combos, before is not None, finish),
        grid=(width // share,),
        in_specs=[pl.BlockSpec(memory_space=pltpu.SMEM)] + specs,
        out_specs=[pl.BlockSpec(shape, lambda n, k=len(shape): (0,) * k) for shape in shapes],
        out_shape=[jax.ShapeDtypeStruct(shape, kind) for shape in shapes],
        scratch_shapes=scratch,
        compiler_params=PARAMS,
        name=name,
    )(core, *arrays)


def home_body(where_ref, pairs_ref, mask_ref, *refs):
    sets, out_ref = (refs[:3], refs[3:6]), refs[6]
    is_k, g = where_ref[0], where_ref[1]
    u, v = pl.program_id(0), pl.program_id(1)
    use = jnp.where(is_k == 1, v, 1 - u)
    i = jnp.where(is_k == 1, u, v)
    quarter = out_ref.shape[2]
    scale = pairs_ref[u, v].astype(jnp.float32).astype(jnp.bfloat16)
    half = quarter // 2
    for q in range(4):
        for at in range(2):
            near, side, far = sets[at]
            bits = q ^ g
            from_side = bits == jnp.where(is_k == 1, 3, 1)
            from_far = bits == jnp.where(is_k == 1, 1, 3)
            for this, ref, lane in (
                ((bits == 0) & (i == 0), near, 0),
                ((bits == 0) & (i == 1), near, 2),
                (from_side & (i == 0), side, 0),
                (from_side & (i == 1), side, 2),
                (from_far, far.at[i], 0),
                (bits == 2, far.at[i], 2),
            ):

                @pl.when((use == at) & this)
                def _():
                    for top in range(2):
                        rows = slice(top * half, (top + 1) * half)
                        lanes = slice(q * quarter, (q + 1) * quarter)
                        tile = ref[:, (lane + top) * quarter : (lane + top + 1) * quarter]
                        out_ref[0, 0, rows, lanes] = tile * (mask_ref[rows, lanes] * scale)


def home(where, pairs, mask, arrays):
    quarter, whole = mask.shape
    full = [pl.BlockSpec(a.shape, lambda u, v, k=a.ndim: (0,) * k) for a in (mask, *arrays)]
    return pl.pallas_call(
        home_body,
        grid=(2, 2),
        in_specs=[pl.BlockSpec(memory_space=pltpu.SMEM)] * 2 + full,
        out_specs=pl.BlockSpec((1, 1, quarter, whole), lambda u, v: (u, v, 0, 0)),
        out_shape=jax.ShapeDtypeStruct((2, 2, quarter, whole), jnp.bfloat16),
        compiler_params=PARAMS,
        name="home",
    )(where, pairs, mask, *arrays)


def local(chol, dressed, pair_mask, sym_mask):
    rows, orbitals, quarter = chol.shape
    occ, g = lax.axis_index("occ"), lax.axis_index("vir")
    core = (occ % NC).astype(jnp.int32).reshape(1)
    order = [centres()]

    turned = [jnp.transpose(a, (1, 0, 2)).reshape(2, PLACES, rows, quarter) for a in (chol, dressed)]
    packed = pack(*turned)
    got = [lax.all_to_all(part, "occ", 0, 0, axis_index_groups=order, tiled=True) for part in packed]

    def spread(k, m):
        k_core = lax.ppermute(k, "occ", core_route())
        k_x = lax.ppermute(k, "vir", x_route(1))
        m_x = lax.ppermute(m, "vir", x_route(3))
        return k_core, k_x, lax.ppermute(k_x, "occ", core_route()), m_x

    near_combos = ((0, 2), (1, 2))
    rest_combos = ((0, 5), (2, 4), (2, 5), (1, 5), (3, 4), (3, 5))

    def near_ops(part, k_core):
        return [(part, 0), k_core, (part, 1)]

    def rest_ops(part, k_core, k_x, k_both, m_x):
        return [(part, 0), k_core, k_x, k_both, (part, 1), m_x]

    one = spread(got[0][:, 0], got[0][:, 1])
    (near,) = tiles("near", quarter, core, near_ops(got[0], one[0]), near_combos)
    two = spread(*split(got[1], near))
    near = tiles("near", quarter, core, near_ops(got[1], two[0]), near_combos, near, finish_near)
    (rest,) = tiles("rest", quarter, core, rest_ops(got[0], *one), rest_combos)
    rest = tiles("rest", quarter, core, rest_ops(got[1], *two), rest_combos, rest, finish_far)

    sent = []
    for is_first in (True, False):
        at = 0 if is_first else 1
        straight, across = home_route(is_first, 0, 0), home_route(is_first, 1, 3)
        axes = ("occ", "vir")
        sent += [
            lax.ppermute(near[at], axes, straight),
            lax.ppermute(rest[at], axes, straight),
            lax.ppermute(rest[2 + at], axes, across),
        ]

    mirror = (occ + PLACES // 2) % PLACES
    pairs = lax.dynamic_slice(pair_mask, (occ * 2, mirror * 2), (2, 2))
    rows_per = quarter // SLAB
    sym_rows = lax.dynamic_slice_in_dim(sym_mask, g * rows_per, rows_per, 0)
    mask = jnp.repeat(jnp.repeat(sym_rows.astype(jnp.bfloat16), SLAB, 0), SLAB, 1)
    where = jnp.stack([(occ < PLACES // 2).astype(jnp.int32), g.astype(jnp.int32)])
    return home(where, pairs, mask, sent)


def solution(mesh):
    placed = (P("occ", None, "vir"), P("occ", None, "vir"), P(), P())
    return jax.shard_map(
        local, mesh=mesh, in_specs=placed, out_specs=P("occ", None, "vir", None), check_vma=False
    )
```

```python
import functools

import jax
import jax.numpy as jnp
from jax import lax
from jax.experimental import pallas as pl
from jax.experimental.pallas import tpu as pltpu
from jax.sharding import PartitionSpec as P

SLAB = 16
NZ, NY, NC = 8, 4, 2
PLACES = NZ * NY * NC
SUB = 8
SHARE = 16
PARAMS = pltpu.CompilerParams(vmem_limit_bytes=48 * 1024 * 1024)


def place(z, y, c):
    return ((z % NZ) * NY + y) * NC + c


def centres():
    return [place(low + 2 + 4 * c, y, r) for low in range(4) for y in range(NY) for c in range(NC) for r in range(2)]


def core_route():
    return [(place(z, y, c), place(z, y, 1 - c)) for z in range(NZ) for y in range(NY) for c in range(NC)]


def x_route(bits):
    return [(g, g ^ bits) for g in range(4)]


def home_route(first, k_bits, m_bits):
    route = []
    for low in range(4):
        for c in range(NC):
            for y in range(NY):
                for r in range(NC):
                    to_k = (r == 0) == first
                    here, there = place(low + 2 + 4 * c, y, r), place(low if to_k else low + 4, y, c)
                    bits = k_bits if to_k else m_bits
                    route += [(here * 4 + g, there * 4 + (g ^ bits)) for g in range(4)]
    return route


def ceil_lanes(lanes):
    return -(-lanes // 128) * 128


def pieces(quarter, groups, at):
    whole = quarter // 128 * 128
    rest = quarter - whole
    cut = [(slice(0, whole), slice(at * whole, (at + 1) * whole))] if whole else []
    start = groups * whole + at * rest
    return cut + ([(slice(whole, quarter), slice(start, start + rest))] if rest else [])


def pack_body(m_lanes, l_ref, x_ref, one_ref, two_ref):
    quarter = l_ref.shape[1]
    spots = one_ref.shape[0]
    turned = []
    for ref in (l_ref, x_ref):
        block = jnp.swapaxes(jnp.swapaxes(ref[...].astype(jnp.float32), 1, 2), 0, 1)
        turned.append(block.astype(jnp.bfloat16).reshape(2, spots, 2, SUB, quarter))
    step = pl.program_id(0)
    n_groups = two_ref.shape[-1] // quarter
    starts = (0, m_lanes // 2, m_lanes)
    for at in range(n_groups):

        @pl.when(step == at)
        def _():
            for r in range(2):
                blocks = (turned[1 - r][1, :, r], turned[r][1, :, r], turned[r][0, :, 0], turned[r][0, :, 1])
                spots_of = [(one_ref, start) for start in starts] + [(two_ref, 0)]
                for block, (ref, start) in zip(blocks, spots_of):
                    for of, to in pieces(quarter, n_groups, at):
                        ref[:, r, :, start + to.start : start + to.stop] = block[:, :, of]


def pack(chol, dressed):
    rows, quarter, orbitals = chol.shape
    spots, groups = orbitals // 4, rows // SUB
    k_lanes = ceil_lanes(groups * quarter)
    m_lanes = 2 * k_lanes
    shapes = [(spots, 2, SUB, m_lanes + k_lanes), (spots, 2, SUB, k_lanes)]
    one, two = pl.pallas_call(
        functools.partial(pack_body, m_lanes),
        grid=(groups,),
        in_specs=[pl.BlockSpec((SUB, quarter, orbitals), lambda n: (n, 0, 0))] * 2,
        out_specs=[pl.BlockSpec(shape, lambda n: (0, 0, 0, 0)) for shape in shapes],
        out_shape=[jax.ShapeDtypeStruct(shape, jnp.bfloat16) for shape in shapes],
        compiler_params=PARAMS,
        name="pack",
    )(chol, dressed)
    return one.reshape(-1, SUB, m_lanes + k_lanes), two.reshape(-1, SUB, k_lanes), k_lanes


def in_lanes(ref, tile):
    high, wide = tile.shape[0] // 4, tile.shape[1]
    for at in range(4):
        ref[:, at * wide : (at + 1) * wide] = tile[at * high : (at + 1) * high].astype(jnp.bfloat16)


def tiles_body(n_left, n_right, messages, quarter, groups, core_ref, *refs):
    lefts, refs = refs[: 2 * n_left], refs[2 * n_left :]
    rights, refs = refs[: 2 * n_right], refs[2 * n_right :]
    firsts, seconds, total = refs[: len(messages)], refs[len(messages) : -1], refs[-1]
    combos = [combo for message in messages for combo in message]
    spots = [(at, n) for at, message in enumerate(messages) for n in range(len(message))]
    step = pl.program_id(0)

    @pl.when(step == 0)
    def _():
        total[...] = jnp.zeros_like(total)

    def rows(ref):
        blocks = []
        for at in range(groups):
            cut = [ref[:, :, to] for _, to in pieces(quarter, groups, at)]
            cut = [part.reshape(-1, part.shape[-1]) for part in cut]
            blocks.append(jnp.concatenate(cut, axis=1) if len(cut) > 1 else cut[0])
        return jnp.concatenate(blocks, axis=0)

    left, right = [
        [jnp.concatenate([rows(own), rows(far)], axis=0) for own, far in zip(side[::2], side[1::2])]
        for side in (lefts, rights)
    ]
    for at, (i, j) in enumerate(combos):
        total[at] += lax.dot_general(left[i], right[j], (((0,), (0,)), ((), ())), preferred_element_type=jnp.float32)

    @pl.when(step == pl.num_programs(0) - 1)
    def _():
        for at, (message, n) in enumerate(spots):
            straight, turned = total[at], total[at].T
            first, second = firsts[message].at[n], seconds[message].at[n]

            @pl.when(core_ref[0] == 0)
            def _():
                in_lanes(first, straight)
                in_lanes(second, turned)

            @pl.when(core_ref[0] == 1)
            def _():
                in_lanes(first, turned)
                in_lanes(second, straight)


def tiles(name, quarter, core, lefts, rights, messages):
    arrays = [a for pair in (*lefts, *rights) for a in pair]
    width = arrays[0].shape[0]
    groups = arrays[0].shape[-1] // quarter
    shapes = [(len(message), quarter // 4, 4 * quarter) for message in messages] * 2
    out = pl.pallas_call(
        functools.partial(tiles_body, len(lefts), len(rights), messages, quarter, groups),
        grid=(width // SHARE,),
        in_specs=[pl.BlockSpec(memory_space=pltpu.SMEM)]
        + [pl.BlockSpec((SHARE, *a.shape[1:]), lambda n: (n, 0, 0)) for a in arrays],
        out_specs=[pl.BlockSpec(shape, lambda n: (0, 0, 0)) for shape in shapes],
        out_shape=[jax.ShapeDtypeStruct(shape, jnp.bfloat16) for shape in shapes],
        scratch_shapes=[pltpu.VMEM((sum(map(len, messages)), quarter, quarter), jnp.float32)],
        compiler_params=PARAMS,
        name=name,
    )(core, *arrays)
    return list(zip(out[: len(messages)], out[len(messages) :]))


def send(pair, k_bits, m_bits):
    return [
        lax.ppermute(pair[at], ("occ", "vir"), home_route(at == 0, k_bits, m_bits)) for at in range(2)
    ]


def home_body(spots, where_ref, pairs_ref, mask_ref, *refs):
    arrived, out_ref, held = refs[:-2], refs[-2], refs[-1]
    is_k, g = where_ref[0], where_ref[1]
    u, v = pl.program_id(0), pl.program_id(1)
    use = jnp.where(is_k == 1, v, 1 - u)
    i = jnp.where(is_k == 1, u, v)
    quarter = out_ref.shape[2]
    scale = pairs_ref[u, v].astype(jnp.float32).astype(jnp.bfloat16)
    for at in range(2):
        for orbital in range(2):

            @pl.when((use == at) & (i == orbital))
            def _():
                for bits in range(4):
                    ref, index = spots[bits, orbital]
                    ref = arrived[2 * ref + at]
                    parts = [ref[index, :, n * quarter : (n + 1) * quarter].astype(jnp.float32) for n in range(4)]
                    held[bits] = jnp.concatenate(parts, axis=0).astype(jnp.bfloat16)

    for q in range(4):
        lanes = slice(q * quarter, (q + 1) * quarter)
        out_ref[0, 0, :, lanes] = held[q ^ g] * (mask_ref[:, lanes] * scale)


def home(spots, where, pairs, mask, arrays):
    quarter, whole = mask.shape
    full = [pl.BlockSpec(a.shape, lambda u, v, k=a.ndim: (0,) * k) for a in (mask, *arrays)]
    return pl.pallas_call(
        functools.partial(home_body, spots),
        grid=(2, 2),
        in_specs=[pl.BlockSpec(memory_space=pltpu.SMEM)] * 2 + full,
        out_specs=pl.BlockSpec((1, 1, quarter, whole), lambda u, v: (u, v, 0, 0)),
        out_shape=jax.ShapeDtypeStruct((2, 2, quarter, whole), jnp.bfloat16),
        scratch_shapes=[pltpu.VMEM((4, quarter, quarter), jnp.bfloat16)],
        compiler_params=PARAMS,
        name="home",
    )(where, pairs, mask, *arrays)


def local(chol, dressed, pair_mask, sym_mask):
    quarter = chol.shape[2]
    occ, g = lax.axis_index("occ"), lax.axis_index("vir")
    core = (occ % NC).astype(jnp.int32).reshape(1)
    order = [centres()]

    def to_core(part):
        return lax.ppermute(part, "occ", core_route())

    def across(part, bits):
        return lax.ppermute(part, "vir", x_route(bits))

    def after(value, *others):
        return lax.optimization_barrier((value, *others))[0]

    one, two, lanes = pack(*[jnp.transpose(a, (0, 2, 1)) for a in (chol, dressed)])
    one = lax.all_to_all(one, "occ", 0, 0, axis_index_groups=order, tiled=True)
    m_own = one[:, :, :lanes]
    one, two, m_own = lax.optimization_barrier((one, two, m_own))
    m_far, k0 = one[:, :, lanes : 2 * lanes], one[:, :, 2 * lanes :]
    k1 = lax.all_to_all(two, "occ", 0, 0, axis_index_groups=order, tiled=True)

    m_own_x = across(m_own, 3)
    near0, far0 = (k0, to_core(k0)), across(k0, 1)
    m = (m_own, m_far)
    (oo0,) = tiles("first", quarter, core, [near0], [m], [[(0, 0)]])
    got_oo0 = send(oo0, 0, 0)

    far0, k1, m_far = lax.optimization_barrier((far0, k1, m_far, m_own_x, *got_oo0))[:3]
    m_x = (m_own_x, across(m_far, 3))
    near1, far1 = (k1, to_core(k1)), across(k1, 1)
    far0 = (far0, to_core(far0))
    (po0,) = tiles("early", quarter, core, [far0], [m], [[(0, 0)]])
    got_po0 = send(po0, 1, 0)
    (oo1,) = tiles("near", quarter, core, [near1], [m], [[(0, 0)]])
    got_oo1 = send(oo1, 0, 0)

    far1 = after(far1, *got_po0, *got_oo1)
    far1 = (far1, to_core(far1))
    m_x = (m_x[0], after(m_x[1], *got_po0, *got_oo1))
    (op,) = tiles("middle", quarter, core, [near0, near1], [m_x], [[(0, 0), (1, 0)]])
    got_op = send(op, 0, 3)
    far1 = (after(far1[0], *op), far1[1])
    pp0, po1, pp1 = tiles("late", quarter, core, [far0, far1], [m, m_x], [[(0, 1)], [(1, 0)], [(1, 1)]])
    got_pp0, got_po1, got_pp1 = send(pp0, 1, 3), send(po1, 1, 0), send(pp1, 1, 3)
    arrived = [*got_oo0, *got_oo1, *got_po0, *got_po1, *got_pp0, *got_pp1, *got_op]
    spots = {(bits, i): (2 * bits + i, 0) for bits in range(3) for i in range(2)}
    spots |= {(3, i): (6, i) for i in range(2)}

    mirror = (occ + PLACES // 2) % PLACES
    pairs = lax.dynamic_slice(pair_mask, (occ * 2, mirror * 2), (2, 2))
    rows_per = quarter // SLAB
    sym_rows = lax.dynamic_slice_in_dim(sym_mask, g * rows_per, rows_per, 0)
    mask = jnp.repeat(jnp.repeat(sym_rows.astype(jnp.bfloat16), SLAB, 0), SLAB, 1)
    where = jnp.stack([(occ < PLACES // 2).astype(jnp.int32), g.astype(jnp.int32)])
    return home(spots, where, pairs, mask, arrived)


def solution(mesh):
    placed = (P("occ", None, "vir"), P("occ", None, "vir"), P(), P())
    return jax.shard_map(
        local, mesh=mesh, in_specs=placed, out_specs=P("occ", None, "vir", None), check_vma=False
    )
```

```python
import functools

import jax
import jax.numpy as jnp
from jax import lax
from jax.experimental import pallas as pl
from jax.experimental.pallas import tpu as pltpu
from jax.sharding import PartitionSpec as P

SLAB = 16
NZ, NY, NC = 8, 4, 2
PLACES = NZ * NY * NC
SUB = 8
SHARE = 16
PARAMS = pltpu.CompilerParams(vmem_limit_bytes=48 * 1024 * 1024)


def place(z, y, c):
    return ((z % NZ) * NY + y) * NC + c


def centres():
    return [place(low + 2 + 4 * c, y, r) for low in range(4) for y in range(NY) for c in range(NC) for r in range(2)]


def core_route():
    return [(place(z, y, c), place(z, y, 1 - c)) for z in range(NZ) for y in range(NY) for c in range(NC)]


def x_route(bits):
    return [(g, g ^ bits) for g in range(4)]


def home_route(first, k_bits, m_bits):
    route = []
    for low in range(4):
        for c in range(NC):
            for y in range(NY):
                for r in range(NC):
                    to_k = (r == 0) == first
                    here, there = place(low + 2 + 4 * c, y, r), place(low if to_k else low + 4, y, c)
                    bits = k_bits if to_k else m_bits
                    route += [(here * 4 + g, there * 4 + (g ^ bits)) for g in range(4)]
    return route


def ceil_lanes(lanes):
    return -(-lanes // 128) * 128


def pieces(quarter, groups, at):
    whole = quarter // 128 * 128
    rest = quarter - whole
    cut = [(slice(0, whole), slice(at * whole, (at + 1) * whole))] if whole else []
    start = groups * whole + at * rest
    return cut + ([(slice(whole, quarter), slice(start, start + rest))] if rest else [])


def pack_body(l_ref, x_ref, m_ref, *k_refs):
    quarter = l_ref.shape[1]
    spots, half = m_ref.shape[0], m_ref.shape[-1] // 2
    turned = []
    for ref in (l_ref, x_ref):
        block = jnp.swapaxes(jnp.swapaxes(ref[...].astype(jnp.float32), 1, 2), 0, 1)
        turned.append(block.astype(jnp.bfloat16).reshape(2, spots, 2, SUB, quarter))
    step = pl.program_id(0)
    n_groups = half // quarter
    for at in range(n_groups):

        @pl.when(step == at)
        def _():
            for r in range(2):
                places = [(turned[1 - r][1, :, r], m_ref, 0), (turned[r][1, :, r], m_ref, half)]
                places += [(turned[r][0, :, i], k_ref, 0) for i, k_ref in enumerate(k_refs)]
                for block, ref, start in places:
                    for of, to in pieces(quarter, n_groups, at):
                        ref[:, r, :, start + to.start : start + to.stop] = block[:, :, of]


def pack(chol, dressed):
    rows, quarter, orbitals = chol.shape
    spots, groups = orbitals // 4, rows // SUB
    lanes = ceil_lanes(groups * quarter)
    shapes = [(spots, 2, SUB, wide) for wide in (2 * lanes, lanes, lanes)]
    out = pl.pallas_call(
        pack_body,
        grid=(groups,),
        in_specs=[pl.BlockSpec((SUB, quarter, orbitals), lambda n: (n, 0, 0))] * 2,
        out_specs=[pl.BlockSpec(shape, lambda n: (0, 0, 0, 0)) for shape in shapes],
        out_shape=[jax.ShapeDtypeStruct(shape, jnp.bfloat16) for shape in shapes],
        compiler_params=PARAMS,
        name="pack",
    )(chol, dressed)
    return [a.reshape(2 * spots, SUB, a.shape[-1]) for a in out], lanes


def in_lanes(ref, tile):
    high, wide = tile.shape[0] // 4, tile.shape[1]
    for at in range(4):
        ref[:, at * wide : (at + 1) * wide] = tile[at * high : (at + 1) * high].astype(jnp.bfloat16)


def tiles_body(n_left, n_right, messages, quarter, groups, core_ref, *refs):
    lefts, refs = refs[: 2 * n_left], refs[2 * n_left :]
    rights, refs = refs[: 2 * n_right], refs[2 * n_right :]
    firsts, seconds, total = refs[: len(messages)], refs[len(messages) : -1], refs[-1]
    combos = [combo for message in messages for combo in message]
    spots = [(at, n) for at, message in enumerate(messages) for n in range(len(message))]
    step = pl.program_id(0)

    @pl.when(step == 0)
    def _():
        total[...] = jnp.zeros_like(total)

    def rows(ref):
        blocks = []
        for at in range(groups):
            cut = [ref[:, :, to] for _, to in pieces(quarter, groups, at)]
            cut = [part.reshape(-1, part.shape[-1]) for part in cut]
            blocks.append(jnp.concatenate(cut, axis=1) if len(cut) > 1 else cut[0])
        return jnp.concatenate(blocks, axis=0)

    left, right = [
        [jnp.concatenate([rows(own), rows(far)], axis=0) for own, far in zip(side[::2], side[1::2])]
        for side in (lefts, rights)
    ]
    for at, (i, j) in enumerate(combos):
        total[at] += lax.dot_general(left[i], right[j], (((0,), (0,)), ((), ())), preferred_element_type=jnp.float32)

    @pl.when(step == pl.num_programs(0) - 1)
    def _():
        for at, (message, n) in enumerate(spots):
            straight, turned = total[at], total[at].T
            first, second = firsts[message].at[n], seconds[message].at[n]

            @pl.when(core_ref[0] == 0)
            def _():
                in_lanes(first, straight)
                in_lanes(second, turned)

            @pl.when(core_ref[0] == 1)
            def _():
                in_lanes(first, turned)
                in_lanes(second, straight)


def tiles(name, quarter, core, lefts, rights, messages):
    ops = [op if isinstance(op, tuple) else (op, 0) for pair in (*lefts, *rights) for op in pair]
    arrays = [array for array, _ in ops]
    width, _, lanes = arrays[0].shape
    groups = lanes // quarter
    shapes = [(len(message), quarter // 4, 4 * quarter) for message in messages] * 2
    out = pl.pallas_call(
        functools.partial(tiles_body, len(lefts), len(rights), messages, quarter, groups),
        grid=(width // SHARE,),
        in_specs=[pl.BlockSpec(memory_space=pltpu.SMEM)]
        + [pl.BlockSpec((SHARE, SUB, lanes), lambda n, half=half: (n, 0, half)) for _, half in ops],
        out_specs=[pl.BlockSpec(shape, lambda n: (0, 0, 0)) for shape in shapes],
        out_shape=[jax.ShapeDtypeStruct(shape, jnp.bfloat16) for shape in shapes],
        scratch_shapes=[pltpu.VMEM((sum(map(len, messages)), quarter, quarter), jnp.float32)],
        compiler_params=PARAMS,
        name=name,
    )(core, *arrays)
    return list(zip(out[: len(messages)], out[len(messages) :]))


def send(pair, k_bits, m_bits):
    return [
        lax.ppermute(pair[at], ("occ", "vir"), home_route(at == 0, k_bits, m_bits)) for at in range(2)
    ]


def home_body(index, where_ref, pairs_ref, mask_ref, *refs):
    arrived, out_ref, held = refs[:-2], refs[-2], refs[-1]
    is_k, g = where_ref[0], where_ref[1]
    u, v = pl.program_id(0), pl.program_id(1)
    use = jnp.where(is_k == 1, v, 1 - u)
    i = jnp.where(is_k == 1, u, v)
    quarter = out_ref.shape[2]
    scale = pairs_ref[u, v].astype(jnp.float32).astype(jnp.bfloat16)
    for at in range(2):
        for orbital in range(2):

            @pl.when((use == at) & (i == orbital))
            def _():
                for bits in range(4):
                    ref = arrived[2 * (4 * orbital + bits) + at]
                    parts = [ref[index[bits, orbital], :, n * quarter : (n + 1) * quarter].astype(jnp.float32) for n in range(4)]
                    held[bits] = jnp.concatenate(parts, axis=0).astype(jnp.bfloat16)

    for q in range(4):
        lanes = slice(q * quarter, (q + 1) * quarter)
        out_ref[0, 0, :, lanes] = held[q ^ g] * (mask_ref[:, lanes] * scale)


def home(index, where, pairs, mask, arrays):
    quarter, whole = mask.shape
    full = [pl.BlockSpec(a.shape, lambda u, v, k=a.ndim: (0,) * k) for a in (mask, *arrays)]
    return pl.pallas_call(
        functools.partial(home_body, index),
        grid=(2, 2),
        in_specs=[pl.BlockSpec(memory_space=pltpu.SMEM)] * 2 + full,
        out_specs=pl.BlockSpec((1, 1, quarter, whole), lambda u, v: (u, v, 0, 0)),
        out_shape=jax.ShapeDtypeStruct((2, 2, quarter, whole), jnp.bfloat16),
        scratch_shapes=[pltpu.VMEM((4, quarter, quarter), jnp.bfloat16)],
        compiler_params=PARAMS,
        name="home",
    )(where, pairs, mask, *arrays)


def local(chol, dressed, pair_mask, sym_mask):
    quarter = chol.shape[2]
    occ, g = lax.axis_index("occ"), lax.axis_index("vir")
    core = (occ % NC).astype(jnp.int32).reshape(1)
    order = [centres()]

    def to_core(part):
        return lax.ppermute(part, "occ", core_route())

    def across(part, bits):
        return lax.ppermute(part, "vir", x_route(bits))

    def after(value, *others):
        return lax.optimization_barrier((value, *others))[0]

    def centre(part):
        return lax.all_to_all(part, "occ", 0, 0, axis_index_groups=order, tiled=True)

    (m, k0, k1), lanes = pack(*[jnp.transpose(a, (0, 2, 1)) for a in (chol, dressed)])
    m, k0, k1 = centre(m), centre(k0), centre(k1)

    m_1, m_3 = across(m, 1), across(m, 3)
    k0 = (k0, to_core(k0))
    ms = {0: ((m, 0), (m, 1))}
    got = {}

    def compute(name, ks, spots):
        messages = [[(left, right) for left in range(len(ks))] for right in range(len(spots))]
        return tiles(name, quarter, core, ks, [ms[q] for q in spots], messages)

    first = compute("first", [k0], [0])
    got[0, 0] = send(first[0], 0, 0)
    m_1, m_3 = lax.optimization_barrier((m_1, m_3, *first[0]))[:2]
    ms |= {1: ((m_1, 0), (m_1, 1)), 3: ((m_3, 0), (m_3, 1))}
    m_2 = m_3[:, :, :lanes], m_1[:, :, lanes:]
    k0_own, *m_2 = lax.optimization_barrier((k0[0], *m_2))
    m_2 = across(m_2[0], 1), across(m_2[1], 3)
    k0 = (k0_own, k0[1])
    second = compute("second", [k0], [1, 3])
    got[1, 0], got[3, 0] = send(second[0], 0, 1), send(second[1], 0, 3)
    k1 = after(k1, *second[0])
    k1 = (k1, to_core(k1))
    third = compute("third", [k1], [0, 1, 3])
    for q, message in zip((0, 1, 3), third):
        got[q, 1] = send(message, 0, q)
    ms[2] = lax.optimization_barrier((*m_2, *got[0, 0], *got[1, 0], *got[3, 0], *got[0, 1]))[:2]
    fourth = compute("fourth", [k0, k1], [2])
    got[2, 0] = got[2, 1] = send(fourth[0], 0, 2)
    arrived = [a for i in range(2) for q in range(4) for a in got[q, i]]
    index = {(q, i): i if q == 2 else 0 for q in range(4) for i in range(2)}

    mirror = (occ + PLACES // 2) % PLACES
    pairs = lax.dynamic_slice(pair_mask, (occ * 2, mirror * 2), (2, 2))
    rows_per = quarter // SLAB
    sym_rows = lax.dynamic_slice_in_dim(sym_mask, g * rows_per, rows_per, 0)
    mask = jnp.repeat(jnp.repeat(sym_rows.astype(jnp.bfloat16), SLAB, 0), SLAB, 1)
    where = jnp.stack([(occ < PLACES // 2).astype(jnp.int32), g.astype(jnp.int32)])
    return home(index, where, pairs, mask, arrived)


def solution(mesh):
    placed = (P("occ", None, "vir"), P("occ", None, "vir"), P(), P())
    return jax.shard_map(
        local, mesh=mesh, in_specs=placed, out_specs=P("occ", None, "vir", None), check_vma=False
    )
```

```python
import functools

import jax
import jax.numpy as jnp
from jax import lax
from jax.experimental import pallas as pl
from jax.experimental.pallas import tpu as pltpu
from jax.sharding import PartitionSpec as P

SLAB = 16
NZ, NY, NC = 8, 4, 2
PLACES = NZ * NY * NC
SUB = 8
SHARE = 16
PARAMS = pltpu.CompilerParams(vmem_limit_bytes=48 * 1024 * 1024)


def place(z, y, c):
    return ((z % NZ) * NY + y) * NC + c


def centres():
    return [place(low + 2 + 4 * c, y, r) for low in range(4) for y in range(NY) for c in range(NC) for r in range(2)]


def core_route():
    return [(place(z, y, c), place(z, y, 1 - c)) for z in range(NZ) for y in range(NY) for c in range(NC)]


def x_route(bits):
    return [(g, g ^ bits) for g in range(4)]


def home_route(first, k_bits, m_bits):
    route = []
    for low in range(4):
        for c in range(NC):
            for y in range(NY):
                for r in range(NC):
                    to_k = (r == 0) == first
                    here, there = place(low + 2 + 4 * c, y, r), place(low if to_k else low + 4, y, c)
                    bits = k_bits if to_k else m_bits
                    route += [(here * 4 + g, there * 4 + (g ^ bits)) for g in range(4)]
    return route


def ceil_lanes(lanes):
    return -(-lanes // 128) * 128


def pieces(quarter, groups, at):
    whole = quarter // 128 * 128
    rest = quarter - whole
    cut = [(slice(0, whole), slice(at * whole, (at + 1) * whole))] if whole else []
    start = groups * whole + at * rest
    return cut + ([(slice(whole, quarter), slice(start, start + rest))] if rest else [])


def pack_body(l_ref, x_ref, m_ref, k_ref):
    quarter = l_ref.shape[1]
    spots, half = m_ref.shape[0], m_ref.shape[-1] // 2
    turned = []
    for ref in (l_ref, x_ref):
        block = jnp.swapaxes(jnp.swapaxes(ref[...], 1, 2).astype(jnp.float32), 0, 1)
        turned.append(block.astype(jnp.bfloat16).reshape(2, spots, 2, SUB, quarter))
    step = pl.program_id(0)
    n_groups = half // quarter
    for at in range(n_groups):

        @pl.when(step == at)
        def _():
            for r in range(2):
                places = [(turned[1 - r][1, :, r], m_ref, 0), (turned[r][1, :, r], m_ref, half)]
                places += [(turned[r][0, :, i], k_ref, i * half) for i in range(2)]
                for block, ref, start in places:
                    for of, to in pieces(quarter, n_groups, at):
                        ref[:, r, :, start + to.start : start + to.stop] = block[:, :, of]


def pack(chol, dressed):
    rows, quarter, orbitals = chol.shape
    spots, groups = orbitals // 4, rows // SUB
    lanes = ceil_lanes(groups * quarter)
    shapes = [(spots, 2, SUB, wide) for wide in (2 * lanes, 2 * lanes)]
    out = pl.pallas_call(
        pack_body,
        grid=(groups,),
        in_specs=[pl.BlockSpec((SUB, quarter, orbitals), lambda n: (n, 0, 0))] * 2,
        out_specs=[pl.BlockSpec(shape, lambda n: (0, 0, 0, 0)) for shape in shapes],
        out_shape=[jax.ShapeDtypeStruct(shape, jnp.bfloat16) for shape in shapes],
        compiler_params=PARAMS,
        name="pack",
    )(chol, dressed)
    return [a.reshape(2 * spots, SUB, a.shape[-1]) for a in out], lanes


def in_lanes(ref, tile):
    high, wide = tile.shape[0] // 4, tile.shape[1]
    for at in range(4):
        ref[:, at * wide : (at + 1) * wide] = tile[at * high : (at + 1) * high].astype(jnp.bfloat16)


def tiles_body(n_left, n_right, messages, quarter, groups, core_ref, *refs):
    lefts, refs = refs[: 2 * n_left], refs[2 * n_left :]
    rights, refs = refs[: 2 * n_right], refs[2 * n_right :]
    firsts, seconds, total = refs[: len(messages)], refs[len(messages) : -1], refs[-1]
    combos = [combo for message in messages for combo in message]
    spots = [(at, n) for at, message in enumerate(messages) for n in range(len(message))]
    step = pl.program_id(0)

    @pl.when(step == 0)
    def _():
        total[...] = jnp.zeros_like(total)

    def rows(ref):
        blocks = []
        for at in range(groups):
            cut = [ref[:, :, to] for _, to in pieces(quarter, groups, at)]
            cut = [part.reshape(-1, part.shape[-1]) for part in cut]
            blocks.append(jnp.concatenate(cut, axis=1) if len(cut) > 1 else cut[0])
        return jnp.concatenate(blocks, axis=0)

    left, right = [
        [jnp.concatenate([rows(own), rows(far)], axis=0) for own, far in zip(side[::2], side[1::2])]
        for side in (lefts, rights)
    ]
    for at, (i, j) in enumerate(combos):
        total[at] += lax.dot_general(left[i], right[j], (((0,), (0,)), ((), ())), preferred_element_type=jnp.float32)

    @pl.when(step == pl.num_programs(0) - 1)
    def _():
        for at, (message, n) in enumerate(spots):
            straight, turned = total[at], total[at].T
            first, second = firsts[message].at[n], seconds[message].at[n]

            @pl.when(core_ref[0] == 0)
            def _():
                in_lanes(first, straight)
                in_lanes(second, turned)

            @pl.when(core_ref[0] == 1)
            def _():
                in_lanes(first, turned)
                in_lanes(second, straight)


def tiles(name, quarter, core, lefts, rights, messages):
    ops = [op if isinstance(op, tuple) else (op, 0) for pair in (*lefts, *rights) for op in pair]
    arrays = [array for array, _ in ops]
    width, lanes = arrays[0].shape[0], arrays[0].shape[-1] // 2
    groups = lanes // quarter
    shapes = [(len(message), quarter // 4, 4 * quarter) for message in messages] * 2
    out = pl.pallas_call(
        functools.partial(tiles_body, len(lefts), len(rights), messages, quarter, groups),
        grid=(width // SHARE,),
        in_specs=[pl.BlockSpec(memory_space=pltpu.SMEM)]
        + [pl.BlockSpec((SHARE, SUB, lanes), lambda n, half=half: (n, 0, half)) for _, half in ops],
        out_specs=[pl.BlockSpec(shape, lambda n: (0, 0, 0)) for shape in shapes],
        out_shape=[jax.ShapeDtypeStruct(shape, jnp.bfloat16) for shape in shapes],
        scratch_shapes=[pltpu.VMEM((sum(map(len, messages)), quarter, quarter), jnp.float32)],
        compiler_params=PARAMS,
        name=name,
    )(core, *arrays)
    return list(zip(out[: len(messages)], out[len(messages) :]))


def send(pair, k_bits, m_bits):
    return [
        lax.ppermute(pair[at], ("occ", "vir"), home_route(at == 0, k_bits, m_bits)) for at in range(2)
    ]


def home_body(where_ref, pairs_ref, mask_ref, *refs):
    arrived, out_ref, held = refs[:-2], refs[-2], refs[-1]
    is_k, g = where_ref[0], where_ref[1]
    u, v = pl.program_id(0), pl.program_id(1)
    use = jnp.where(is_k == 1, v, 1 - u)
    i = jnp.where(is_k == 1, u, v)
    quarter = out_ref.shape[2]
    scale = pairs_ref[u, v].astype(jnp.float32).astype(jnp.bfloat16)
    for at in range(2):
        for orbital in range(2):

            @pl.when((use == at) & (i == orbital))
            def _():
                for bits in range(4):
                    ref = arrived[2 * bits + at]
                    parts = [ref[orbital, :, n * quarter : (n + 1) * quarter].astype(jnp.float32) for n in range(4)]
                    held[bits] = jnp.concatenate(parts, axis=0).astype(jnp.bfloat16)

    for q in range(4):
        lanes = slice(q * quarter, (q + 1) * quarter)
        out_ref[0, 0, :, lanes] = held[q ^ g] * (mask_ref[:, lanes] * scale)


def home(where, pairs, mask, arrays):
    quarter, whole = mask.shape
    full = [pl.BlockSpec(a.shape, lambda u, v, k=a.ndim: (0,) * k) for a in (mask, *arrays)]
    return pl.pallas_call(
        home_body,
        grid=(2, 2),
        in_specs=[pl.BlockSpec(memory_space=pltpu.SMEM)] * 2 + full,
        out_specs=pl.BlockSpec((1, 1, quarter, whole), lambda u, v: (u, v, 0, 0)),
        out_shape=jax.ShapeDtypeStruct((2, 2, quarter, whole), jnp.bfloat16),
        scratch_shapes=[pltpu.VMEM((4, quarter, quarter), jnp.bfloat16)],
        compiler_params=PARAMS,
        name="home",
    )(where, pairs, mask, *arrays)


def local(chol, dressed, pair_mask, sym_mask):
    quarter = chol.shape[2]
    occ, g = lax.axis_index("occ"), lax.axis_index("vir")
    core = (occ % NC).astype(jnp.int32).reshape(1)
    order = [centres()]

    def to_core(part):
        return lax.ppermute(part, "occ", core_route())

    def across(part, bits):
        return lax.ppermute(part, "vir", x_route(bits))

    def after(value, *others):
        return lax.optimization_barrier((value, *others))[0]

    def centre(part):
        return lax.all_to_all(part, "occ", 0, 0, axis_index_groups=order, tiled=True)

    (m, k), lanes = pack(*[jnp.transpose(a, (0, 2, 1)) for a in (chol, dressed)])
    m, k = centre(m), centre(k)

    m_1, m_3 = across(m, 1), across(m, 3)
    m_2 = across(m_3[:, :, :lanes], 1), across(m_1[:, :, lanes:], 3)
    k_core = to_core(k)
    ks = [((k, i), (k_core, i)) for i in range(2)]
    ms = {q: ((array, 0), (array, 1)) for q, array in ((0, m), (1, m_1), (3, m_3))}
    got = {}

    def compute(name, spots):
        messages = [[(left, right) for left in range(2)] for right in range(len(spots))]
        return tiles(name, quarter, core, ks, [ms[q] for q in spots], messages)

    (first,) = compute("first", [0])
    got[0] = send(first, 0, 0)
    m_1, m_3 = lax.optimization_barrier((m_1, m_3, *first))[:2]
    ms |= {1: ((m_1, 0), (m_1, 1)), 3: ((m_3, 0), (m_3, 1))}
    second = compute("second", [1, 3])
    got[1], got[3] = send(second[0], 0, 1), send(second[1], 0, 3)
    ms[2] = lax.optimization_barrier((*m_2, *got[0], *second[0]))[:2]
    (third,) = compute("third", [2])
    got[2] = send(third, 0, 2)
    arrived = [a for q in range(4) for a in got[q]]

    mirror = (occ + PLACES // 2) % PLACES
    pairs = lax.dynamic_slice(pair_mask, (occ * 2, mirror * 2), (2, 2))
    rows_per = quarter // SLAB
    sym_rows = lax.dynamic_slice_in_dim(sym_mask, g * rows_per, rows_per, 0)
    mask = jnp.repeat(jnp.repeat(sym_rows.astype(jnp.bfloat16), SLAB, 0), SLAB, 1)
    where = jnp.stack([(occ < PLACES // 2).astype(jnp.int32), g.astype(jnp.int32)])
    return home(where, pairs, mask, arrived)


def solution(mesh):
    placed = (P("occ", None, "vir"), P("occ", None, "vir"), P(), P())
    return jax.shard_map(
        local, mesh=mesh, in_specs=placed, out_specs=P("occ", None, "vir", None), check_vma=False
    )
```
